32 devices in a mesh: snap: 4 (over y, core), vtx: 8 (over z, x).
Axes of the slice: x: 2, y: 2, z: 4, core: 2. Of those that a mesh axis runs over, the one named last changes fastest.
Arguments:
- features: bfloat16 [8, 8192, 128], P('snap', 'vtx'), may hold values from -6 to 6
- tile_vals: bfloat16 [8, 64, 8, 128, 128], P('snap', 'vtx'), may hold values from -0.25 to 0.25
- tile_cols: int32 [8, 64, 8], P('snap', 'vtx'), may hold values from 0 to 63, as said below
- tile_count: int32 [8, 64], P('snap', 'vtx'), may hold values from 1 to 8
- gcn_weight: bfloat16 [128, 128], replicated, may hold values from -0.5 to 0.5
- gcn_bias: float32 [128], replicated, may hold values from -3 to 3
- input_weight: bfloat16 [128, 512], replicated, may hold values from -0.5 to 0.5
- recur_weight: bfloat16 [128, 512], replicated, may hold values from -0.5 to 0.5
- lstm_bias: float32 [512], replicated, may hold values from -4 to 4
- hidden_grad: bfloat16 [8, 1024, 8, 128], P('vtx', 'snap'), may hold values from -6 to 6
Outputs:
- hidden_states: bfloat16 [8, 1024, 8, 128], P('vtx', 'snap')
- grad_gcn_weight: float32 [128, 128], replicated
- grad_gcn_bias: float32 [128], replicated
- grad_input_weight: float32 [128, 512], replicated
- grad_recur_weight: float32 [128, 512], replicated
- grad_lstm_bias: float32 [512], replicated
The draws below stay inside these ranges and needn't reach their ends.
Inputs may be any that keep to these rules, and one draw needn't show every extreme that they name: `tile_cols`: within one snapshot, the 8 slots of one row block name distinct column blocks, and all slots, live or not, of the row blocks j * 8 to (j + 1) * 8 - 1 together name at most one block of each group of 8 consecutive blocks.
All inputs are finite; a program needn't handle non-finite values.
Results may differ from the reference program's by a relative error of at most 0.0085.
Values may be sent and summed in bfloat16 or wider, within the bound.
A program may use at most 128 MiB of HBM per device.

```python
import jax
import jax.numpy as jnp
from jax import lax

F = 128
HID = 128
TILE = 128
VB_DEV = 8
MAXB = 8
NBLK = 64
V = 8192
SNAPS = 8
N_VTX = 8


def draw_tile_cols(key, part):
    key_order = jax.random.fold_in(key, 11)
    key_pick = jax.random.fold_in(key, 12)
    scores = jax.random.randint(key_order, (SNAPS, NBLK, N_VTX), 0, 2 ** 20) * N_VTX + jnp.arange(N_VTX, dtype=jnp.int32)
    peer_order = jnp.argsort(scores, axis=2)[:, :, :MAXB].astype(jnp.int32)
    picks = jax.random.randint(key_pick, (SNAPS, N_VTX, N_VTX), 0, VB_DEV)
    holder = jnp.arange(NBLK, dtype=jnp.int32) // VB_DEV
    picked_rows = picks[:, holder, :]
    chosen = jnp.take_along_axis(picked_rows, peer_order, axis=2)
    return (peer_order * VB_DEV + chosen).astype(jnp.int32)


def draw_tile_count(key, part):
    key_level = jax.random.fold_in(key, 21)
    key_count = jax.random.fold_in(key, 22)
    key_spot = jax.random.fold_in(key, 23)
    levels = jax.random.randint(key_level, (SNAPS, N_VTX), MAXB // 2, MAXB + 1)
    holder = jnp.arange(NBLK, dtype=jnp.int32) // VB_DEV
    ceiling = levels[:, holder]
    counts = jax.random.randint(key_count, (SNAPS, NBLK), 0, 2 ** 20) % ceiling + 1
    spot = jax.random.randint(key_spot, (), 0, SNAPS * NBLK)
    counts = counts.reshape(-1).at[spot].set(MAXB).reshape(SNAPS, NBLK)
    return counts.astype(jnp.int32)


def steps_of(rng, extent, cuts, least, top_value):
    loudness, own = 1.0, jax.random.fold_in(rng, 6)
    for axis_at, blocks in cuts:
        heights = jnp.exp(jax.random.uniform(jax.random.fold_in(own, axis_at), (blocks,), jnp.float32, least / len(cuts), top_value / len(cuts)))
        loudness = loudness * jnp.repeat(heights, extent[axis_at] // blocks).reshape([-1 if axis == axis_at else 1 for axis in range(len(extent))])
    return loudness


def bell_draw(own_key, shape, scale, reach, split=(), held_as=jnp.bfloat16):
    values = jax.random.normal(own_key, shape, jnp.float32) * scale
    if len(split) > 0:
        values = steps_of(own_key, shape, split, -0.22, 0.18) * values
    return jnp.clip(values, min=-reach, max=reach).astype(held_as)


def setup_inputs(seed: int = 0) -> dict:
    seeds = jax.random.split(jax.random.key(seed), 11)
    features = bell_draw(seeds[0], (SNAPS, V, F), 1.0, 6.0, ((0, 4), (1, 8)))
    tile_vals = bell_draw(seeds[1], (SNAPS, NBLK, MAXB, TILE, TILE), (TILE * 4) ** -0.5, 0.25, ((0, 4), (1, 8)))
    tile_cols = draw_tile_cols(jax.random.fold_in(seeds[10], 71), 0)
    tile_count = draw_tile_count(jax.random.fold_in(seeds[10], 71), 0)
    gcn_weight = bell_draw(seeds[4], (F, F), F ** -0.5, 0.5)
    gcn_bias = bell_draw(seeds[5], (F,), 0.5, 3.0, (), jnp.float32)
    input_weight = bell_draw(seeds[6], (F, 4 * HID), F ** -0.5, 0.5)
    recur_weight = bell_draw(seeds[7], (HID, 4 * HID), HID ** -0.5, 0.5)
    lstm_bias = bell_draw(seeds[8], (4 * HID,), 1.0, 4.0, (), jnp.float32)
    hidden_grad = bell_draw(seeds[9], (N_VTX, VB_DEV * TILE, SNAPS, HID), 1.0, 6.0, ((0, 8), (1, 4)))
    return {"features": features, "tile_vals": tile_vals, "tile_cols": tile_cols, "tile_count": tile_count, "gcn_weight": gcn_weight, "gcn_bias": gcn_bias, "input_weight": input_weight, "recur_weight": recur_weight, "lstm_bias": lstm_bias, "hidden_grad": hidden_grad}


def aggregate_snapshot(packed):
    feats, tiles, cols, counts = packed
    blocks = feats.reshape(NBLK, TILE, F)
    live_mask = jnp.arange(MAXB, dtype=jnp.int32)[None, :] < counts[:, None]
    fetched = jnp.where(live_mask[:, :, None, None], blocks[cols], 0).astype(jnp.float32)
    summed = jnp.einsum('rmij,rmjf->rif', tiles.astype(jnp.float32), fetched)
    return summed.astype(jnp.bfloat16).reshape(NBLK * TILE, F)


def reference(features, tile_vals, tile_cols, tile_count, gcn_weight, gcn_bias, input_weight, recur_weight, lstm_bias, hidden_grad):
    aggregated = lax.map(aggregate_snapshot, (features, tile_vals, tile_cols, tile_count))
    flat_agg = aggregated.reshape(SNAPS * V, F)
    pre_act = jnp.dot(flat_agg, gcn_weight, preferred_element_type=jnp.float32) + gcn_bias
    layer_out = jax.nn.silu(pre_act).astype(jnp.bfloat16)
    layer_seq = layer_out.reshape(SNAPS, V, F)

    def advance(carried, layer_step):
        cell_state, last_out = carried
        input_gates = jnp.dot(layer_step, input_weight, preferred_element_type=jnp.float32) + lstm_bias
        pre_gates = input_gates + jnp.dot(last_out, recur_weight, preferred_element_type=jnp.float32)
        gate_in = jax.nn.sigmoid(pre_gates[:, :HID])
        gate_keep = jax.nn.sigmoid(pre_gates[:, HID:2 * HID])
        gate_new = jnp.tanh(pre_gates[:, 2 * HID:3 * HID])
        gate_out = jax.nn.sigmoid(pre_gates[:, 3 * HID:])
        cell_state = gate_keep * cell_state + gate_in * gate_new
        new_out = (gate_out * jnp.tanh(cell_state)).astype(jnp.bfloat16)
        return (cell_state, new_out), (pre_gates, cell_state, new_out)

    start = (jnp.zeros((V, HID), jnp.float32), jnp.zeros((V, HID), jnp.bfloat16))
    _, (all_pre, all_cells, all_outs) = lax.scan(advance, start, layer_seq)
    prev_cells = jnp.concatenate([jnp.zeros((1, V, HID), jnp.float32), all_cells[:-1]], axis=0)
    prev_outs = jnp.concatenate([jnp.zeros((1, V, HID), jnp.bfloat16), all_outs[:-1]], axis=0)
    grad_outs = hidden_grad.reshape(V, SNAPS, HID).transpose(1, 0, 2).astype(jnp.float32)

    def retreat(carried, step_items):
        grad_cell, grad_back = carried
        pre_gates, cell_state, prev_cell, grad_out = step_items
        gate_in = jax.nn.sigmoid(pre_gates[:, :HID])
        gate_keep = jax.nn.sigmoid(pre_gates[:, HID:2 * HID])
        gate_new = jnp.tanh(pre_gates[:, 2 * HID:3 * HID])
        gate_out = jax.nn.sigmoid(pre_gates[:, 3 * HID:])
        squash = jnp.tanh(cell_state)
        grad_total = grad_out + grad_back
        grad_cell = grad_cell + grad_total * gate_out * (1.0 - squash * squash)
        grad_gates = jnp.concatenate([
            grad_cell * gate_new * gate_in * (1.0 - gate_in),
            grad_cell * prev_cell * gate_keep * (1.0 - gate_keep),
            grad_cell * gate_in * (1.0 - gate_new * gate_new),
            grad_total * squash * gate_out * (1.0 - gate_out)], axis=1).astype(jnp.bfloat16)
        grad_back = jnp.einsum('rg,hg->rh', grad_gates, recur_weight, preferred_element_type=jnp.float32)
        return (grad_cell * gate_keep, grad_back), grad_gates

    _, all_grad_gates = lax.scan(retreat, (jnp.zeros((V, HID), jnp.float32), jnp.zeros((V, HID), jnp.float32)), (all_pre, all_cells, prev_cells, grad_outs), reverse=True)
    flat_gates = all_grad_gates.reshape(SNAPS * V, 4 * HID)
    grad_input = jnp.einsum('rf,rg->fg', layer_out, flat_gates, preferred_element_type=jnp.float32)
    grad_recur = jnp.einsum('rh,rg->hg', prev_outs.reshape(SNAPS * V, HID), flat_gates, preferred_element_type=jnp.float32)
    grad_bias = jnp.sum(flat_gates.astype(jnp.float32), axis=0)
    grad_layer = jnp.einsum('rg,fg->rf', flat_gates, input_weight, preferred_element_type=jnp.float32).astype(jnp.bfloat16)
    squeeze = jax.nn.sigmoid(pre_act)
    grad_pre = (grad_layer.astype(jnp.float32) * squeeze * (1.0 + pre_act * (1.0 - squeeze))).astype(jnp.bfloat16)
    grad_gcn = jnp.einsum('rf,rg->fg', flat_agg, grad_pre, preferred_element_type=jnp.float32)
    grad_gbias = jnp.sum(grad_pre.astype(jnp.float32), axis=0)
    hidden_states = all_outs.transpose(1, 0, 2).reshape(N_VTX, V // N_VTX, SNAPS, HID)
    return (hidden_states, grad_gcn, grad_gbias, grad_input, grad_recur, grad_bias)
```

```python
import functools

import jax
import jax.numpy as jnp
from jax import lax
from jax.experimental import pallas as pl
from jax.experimental.pallas import tpu as pltpu
from jax.sharding import PartitionSpec as P

MESH = pl.DeviceIdType.MESH
LANES = 128


def sigmoid(x):
    return 0.5 * jnp.tanh(0.5 * x) + 0.5


class Reducer:
    def __init__(self, me, sizes, own, part_in, part_sum, chunk_in, whole, sems):
        self.me, self.sizes = me, sizes
        self.own, self.part_in, self.part_sum = own, part_in, part_sum
        self.chunk_in, self.whole, self.sems = chunk_in, whole, sems
        self.part = part_sum.shape[0]
        self.chunk = self.part // sizes["vtx"]

    def rows(self, snap, vtx=None):
        if vtx is None:
            return pl.ds(pl.multiple_of(snap * self.part, self.part), self.part)
        return pl.ds(pl.multiple_of(snap * self.part + vtx * self.chunk, self.chunk), self.chunk)

    def copy(self, stage, k, forward):
        axis = ("snap", "vtx", "vtx", "snap")[stage]
        n, me = self.sizes[axis], self.me[axis]
        peer = lax.rem(me + k, n) if forward else lax.rem(me - k + n, n)
        if stage == 0:
            src, dst = self.own.at[self.rows(peer)], self.part_in.at[k - 1]
        elif stage == 1:
            here = pl.ds(pl.multiple_of(peer * self.chunk, self.chunk), self.chunk)
            src, dst = self.part_sum.at[here], self.chunk_in.at[k - 1]
        elif stage == 2:
            src = dst = self.whole.at[self.rows(self.me["snap"], me if forward else peer)]
        else:
            src = dst = self.whole.at[self.rows(me if forward else peer)]
        return pltpu.make_async_remote_copy(
            src_ref=src,
            dst_ref=dst,
            send_sem=self.sems.at[2 * stage, k],
            recv_sem=self.sems.at[2 * stage + 1, k],
            device_id={axis: peer},
            device_id_type=MESH,
        )

    def peers(self, stage):
        return range(1, self.sizes[("snap", "vtx", "vtx", "snap")[stage]])

    def start(self, stage):
        for k in self.peers(stage):
            self.copy(stage, k, True).start()

    def finish(self, stage):
        for k in self.peers(stage):
            self.copy(stage, k, False).wait_recv()
        if stage == 0:
            total = self.own[self.rows(self.me["snap"]), :]
            for k in self.peers(stage):
                total = total + self.part_in[k - 1].astype(jnp.float32)
            self.part_sum[...] = total
        elif stage == 1:
            here = pl.ds(pl.multiple_of(self.me["vtx"] * self.chunk, self.chunk), self.chunk)
            total = self.part_sum[here, :]
            for k in self.peers(stage):
                total = total + self.chunk_in[k - 1].astype(jnp.float32)
            place = self.rows(self.me["snap"], self.me["vtx"])
            self.whole[place, :] = total.astype(self.whole.dtype)

    def drain(self):
        for stage in range(4):
            for k in self.peers(stage):
                self.copy(stage, k, True).wait_send()


def kernel(
    sizes,
    request_ref,
    place_ref,
    feat_ref,
    tiles_ref,
    gcn_w_ref,
    gcn_b_ref,
    in_w_ref,
    rec_w_ref,
    lstm_b_ref,
    hgrad_ref,
    hid_out,
    gcn_out,
    gcn_b_out,
    in_out,
    rec_out,
    lstm_b_out,
    tiles,
    asked,
    staged,
    fetched,
    aggregated,
    pre_act,
    layer,
    xs,
    hs,
    acts,
    cells,
    dlayer,
    dlayer_in,
    dcell,
    back,
    weights,
    weights_t,
    lstm_b_sum,
    sum1,
    part_in1,
    part1,
    chunk_in1,
    whole1,
    sum2,
    part_in2,
    part2,
    chunk_in2,
    whole2,
    tile_sem,
    ask_sem,
    feat_sem,
    layer_sem,
    back_send,
    back_recv,
    sems1,
    sems2,
):
    ns, nv = sizes["snap"], sizes["vtx"]
    me_s, me_v = lax.axis_index("snap"), lax.axis_index("vtx")
    me = {"snap": me_s, "vtx": me_v}
    steps, verts, width = layer.shape
    _, row_blocks, slots, tile, _ = tiles_ref.shape
    total_steps, rows, hid = hgrad_ref.shape

    def remote(src, dst, send, recv, axis, peer):
        return pltpu.make_async_remote_copy(
            src_ref=src,
            dst_ref=dst,
            send_sem=send,
            recv_sem=recv,
            device_id={axis: peer},
            device_id_type=MESH,
        )

    barrier = pltpu.get_barrier_semaphore()
    for axis in ("snap", "vtx"):
        for k in range(1, sizes[axis]):
            peer = lax.rem(me[axis] + k, sizes[axis])
            pl.semaphore_signal(barrier, inc=1, device_id={axis: peer}, device_id_type=MESH)
    load_tiles = pltpu.make_async_copy(tiles_ref, tiles, tile_sem)
    load_tiles.start()
    fetched[nv] = jnp.zeros((steps, tile, width), jnp.bfloat16)
    weights[...] = jnp.concatenate([in_w_ref[...], rec_w_ref[...]], axis=0)
    weights_t[...] = weights[...].T
    pl.semaphore_wait(barrier, ns + nv - 2)

    def ask(k, forward):
        peer = lax.rem(me_v + k, nv) if forward else lax.rem(me_v - k + nv, nv)
        return remote(
            request_ref.at[peer], asked.at[k], ask_sem.at[0, k], ask_sem.at[1, k], "vtx", peer
        )

    def give(k, forward):
        peer = lax.rem(me_v + k, nv) if forward else lax.rem(me_v - k + nv, nv)
        return remote(
            staged.at[k],
            fetched.at[me_v if forward else peer],
            feat_sem.at[0, k],
            feat_sem.at[1, k],
            "vtx",
            peer,
        )

    for k in range(1, nv):
        ask(k, True).start()
    own_request = request_ref[me_v]
    for s in range(steps):
        fetched[me_v, s] = feat_ref[s, own_request[s, 0]]
    for k in range(1, nv):
        ask(nv - k, False).wait_recv()
        wanted = asked[nv - k]
        for s in range(steps):
            staged[k, s] = feat_ref[s, wanted[s, 0]]
        give(k, True).start()
    for k in range(1, nv):
        give(k, False).wait_recv()
    load_tiles.wait()

    def layer_copy(k, s, forward):
        peer = lax.rem(me_s + k, ns) if forward else lax.rem(me_s - k + ns, ns)
        holder = me_s if forward else peer
        return remote(
            layer.at[s, pl.ds(pl.multiple_of(peer * rows, rows), rows)],
            xs.at[holder * steps + s],
            layer_sem.at[0, k, s],
            layer_sem.at[1, k, s],
            "snap",
            peer,
        )

    def convolve(s, carry):
        for r in range(row_blocks):
            picked = [fetched[place_ref[s, r, m], s] for m in range(slots)]
            left = jnp.concatenate([tiles[s, r, m] for m in range(slots)], axis=1)
            summed = jnp.dot(
                left, jnp.concatenate(picked, axis=0), preferred_element_type=jnp.float32
            )
            aggregated[s, pl.ds(r * tile, tile), :] = summed.astype(jnp.bfloat16)
        pre = (
            jnp.dot(aggregated[s], gcn_w_ref[...], preferred_element_type=jnp.float32)
            + gcn_b_ref[...]
        )
        pre_act[s] = pre
        layer[s] = (pre * sigmoid(pre)).astype(jnp.bfloat16)
        for k in range(1, ns):
            layer_copy(k, s, True).start()
        xs[me_s * steps + s] = layer[s, pl.ds(pl.multiple_of(me_s * rows, rows), rows), :]
        return carry

    lax.fori_loop(0, steps, convolve, 0)

    hs[0] = jnp.zeros((rows, hid), jnp.bfloat16)
    cells[0] = jnp.zeros((rows, hid), jnp.float32)

    def advance(t, carry):
        holder = lax.div(t, steps)

        @pl.when(holder != me_s)
        def _():
            k = lax.rem(me_s - holder + ns, ns)
            layer_copy(k, lax.rem(t, steps), False).wait_recv()

        both = jnp.concatenate([xs[t], hs[t]], axis=1)
        gates = jnp.dot(both, weights[...], preferred_element_type=jnp.float32) + lstm_b_ref[...]
        gate_in = sigmoid(gates[:, :hid])
        gate_keep = sigmoid(gates[:, hid : 2 * hid])
        gate_new = jnp.tanh(gates[:, 2 * hid : 3 * hid])
        gate_out = sigmoid(gates[:, 3 * hid :])
        cell = gate_keep * cells[t] + gate_in * gate_new
        out = (gate_out * jnp.tanh(cell)).astype(jnp.bfloat16)
        acts[t, 0] = gate_in
        acts[t, 1] = gate_keep
        acts[t, 2] = gate_new
        acts[t, 3] = gate_out
        cells[t + 1] = cell
        hs[t + 1] = out
        hid_out[t] = out
        return carry

    lax.fori_loop(0, total_steps, advance, 0)

    def back_copy(t, peer, forward):
        holder = lax.div(t, steps)
        s = lax.rem(t, steps)
        k = lax.rem(holder - me_s + ns, ns) if forward else lax.rem(me_s - peer + ns, ns)
        sender = me_s if forward else peer
        return remote(
            dlayer.at[t],
            dlayer_in.at[s, pl.ds(pl.multiple_of(sender * rows, rows), rows)],
            back_send.at[t],
            back_recv.at[k, s],
            "snap",
            holder if forward else peer,
        )

    dcell[...] = jnp.zeros((rows, hid), jnp.float32)
    back[...] = jnp.zeros((rows, hid), jnp.float32)
    lstm_b_sum[...] = jnp.zeros(lstm_b_sum.shape, jnp.float32)
    sum1[...] = jnp.zeros(sum1.shape, jnp.float32)
    height = width + hid

    def retreat(step, carry):
        t = total_steps - 1 - step
        gate_in, gate_keep, gate_new, gate_out = (acts[t, q] for q in range(4))
        squash = jnp.tanh(cells[t + 1])
        dh = hgrad_ref[t].astype(jnp.float32) + back[...]
        dc = dcell[...] + dh * gate_out * (1.0 - squash * squash)
        dgates = jnp.concatenate(
            [
                dc * gate_new * gate_in * (1.0 - gate_in),
                dc * cells[t] * gate_keep * (1.0 - gate_keep),
                dc * gate_in * (1.0 - gate_new * gate_new),
                dh * squash * gate_out * (1.0 - gate_out),
            ],
            axis=1,
        ).astype(jnp.bfloat16)
        dcell[...] = dc * gate_keep
        both_back = jnp.dot(dgates, weights_t[...], preferred_element_type=jnp.float32)
        back[...] = both_back[:, width:]
        grad = both_back[:, :width].astype(jnp.bfloat16)
        holder = lax.div(t, steps)

        @pl.when(holder != me_s)
        def _():
            dlayer[t] = grad
            back_copy(t, None, True).start()

        @pl.when(holder == me_s)
        def _():
            place = pl.ds(pl.multiple_of(me_s * rows, rows), rows)
            dlayer_in[lax.rem(t, steps), place, :] = grad

        lstm_b_sum[...] += jnp.sum(
            dgates.astype(jnp.float32).reshape(rows // 8, 8, 4 * hid), axis=0
        )
        both = jnp.concatenate([xs[t], hs[t]], axis=1)
        term = lax.dot_general(
            both, dgates, (((0,), (0,)), ((), ())), preferred_element_type=jnp.float32
        )
        for q in range(4):
            sum1[q * height : (q + 1) * height, :] += term[:, q * hid : (q + 1) * hid]
        return carry

    lax.fori_loop(0, total_steps, retreat, 0)

    first = Reducer(me, sizes, sum1, part_in1, part1, chunk_in1, whole1, sems1)
    second = Reducer(me, sizes, sum2, part_in2, part2, chunk_in2, whole2, sems2)
    first.start(0)

    sum2[...] = jnp.zeros(sum2.shape, jnp.float32)
    gcn_b_sum = jnp.zeros((1, width), jnp.float32)
    for s in reversed(range(steps)):
        for k in range(1, ns):
            src = lax.rem(me_s - k + ns, ns)
            back_copy(me_s * steps + s, src, False).wait_recv()
        pre = pre_act[s]
        slope = sigmoid(pre)
        dpre = (dlayer_in[s].astype(jnp.float32) * slope * (1.0 + pre * (1.0 - slope))).astype(
            jnp.bfloat16
        )
        sum2[:width, :] += lax.dot_general(
            aggregated[s], dpre, (((0,), (0,)), ((), ())), preferred_element_type=jnp.float32
        )
        gcn_b_sum = gcn_b_sum + jnp.sum(dpre.astype(jnp.float32), axis=0, keepdims=True)
    lstm_b = jnp.sum(lstm_b_sum[...], axis=0, keepdims=True)
    sum2[width : width + 1, :] = gcn_b_sum
    for q in range(4):
        sum2[width + 1 + q : width + 2 + q, :] = lstm_b[:, q * hid : (q + 1) * hid]

    second.start(0)
    for stage in range(4):
        first.finish(stage)
        if stage < 3:
            first.start(stage + 1)
        second.finish(stage)
        if stage < 3:
            second.start(stage + 1)

    for q in range(4):
        at = q * height
        span = slice(q * hid, (q + 1) * hid)
        in_out[:, span] = whole1[at : at + width, :].astype(jnp.float32)
        rec_out[:, span] = whole1[at + width : at + height, :].astype(jnp.float32)
        lstm_b_out[:, span] = whole2[width + 1 + q : width + 2 + q, :]
    gcn_out[...] = whole2[:width, :]
    gcn_b_out[...] = whole2[width : width + 1, :]

    for k in range(1, nv):
        ask(k, True).wait_send()
        give(k, True).wait_send()
    for k in range(1, ns):
        for s in range(steps):
            layer_copy(k, s, True).wait_send()

    def drain(t, carry):
        @pl.when(lax.div(t, steps) != me_s)
        def _():
            back_copy(t, None, True).wait_send()

        return carry

    lax.fori_loop(0, total_steps, drain, 0)
    first.drain()
    second.drain()


def on_device(
    sizes,
    features,
    tile_vals,
    tile_cols,
    tile_count,
    gcn_weight,
    gcn_bias,
    input_weight,
    recur_weight,
    lstm_bias,
    hidden_grad,
):
    ns, nv = sizes["snap"], sizes["vtx"]
    steps, verts, width = features.shape
    _, row_blocks, slots, tile, _ = tile_vals.shape
    hid = recur_weight.shape[0]
    _, rows, total_steps, _ = hidden_grad.shape
    bf16, f32 = jnp.bfloat16, jnp.float32

    flat = tile_cols.reshape(1, steps, row_blocks * slots)
    low = jnp.arange(nv, dtype=jnp.int32)[:, None, None] * row_blocks
    named = jnp.where((flat >= low) & (flat < low + row_blocks), flat - low, 0)
    request = jnp.max(named, axis=2)
    request = jnp.pad(request, ((0, 0), (0, -steps % 8)))
    request = jnp.broadcast_to(request[:, :, None], request.shape + (LANES,))

    live = lax.broadcasted_iota(jnp.int32, tile_cols.shape, 2) < tile_count[:, :, None]
    places = jnp.where(live, tile_cols // row_blocks, nv)

    def padded(count, unit):
        unit = unit * ns * nv
        return -(-count // unit) * unit

    rows1 = padded(4 * (width + hid), 16)
    rows2 = padded(width + 5, 8)
    most = max(ns, nv)
    dma = pltpu.SemaphoreType.DMA

    def reduction(count, kept):
        part = count // ns
        return [
            pltpu.VMEM((count, LANES), f32),
            pltpu.VMEM((ns - 1, part, LANES), f32),
            pltpu.VMEM((part, LANES), f32),
            pltpu.VMEM((nv - 1, part // nv, LANES), f32),
            pltpu.VMEM((count, LANES), kept),
        ]

    scratch = [
        pltpu.VMEM(tile_vals.shape, bf16),
        pltpu.VMEM((nv,) + request.shape[1:], jnp.int32),
        pltpu.VMEM((nv, steps, tile, width), bf16),
        pltpu.VMEM((nv + 1, steps, tile, width), bf16),
        pltpu.VMEM((steps, verts, width), bf16),
        pltpu.VMEM((steps, verts, width), f32),
        pltpu.VMEM((steps, verts, width), bf16),
        pltpu.VMEM((total_steps, rows, width), bf16),
        pltpu.VMEM((total_steps + 1, rows, hid), bf16),
        pltpu.VMEM((total_steps, 4, rows, hid), f32),
        pltpu.VMEM((total_steps + 1, rows, hid), f32),
        pltpu.VMEM((total_steps, rows, width), bf16),
        pltpu.VMEM((steps, verts, width), bf16),
        pltpu.VMEM((rows, hid), f32),
        pltpu.VMEM((rows, hid), f32),
        pltpu.VMEM((width + hid, 4 * hid), bf16),
        pltpu.VMEM((4 * hid, width + hid), bf16),
        pltpu.VMEM((8, 4 * hid), f32),
        *reduction(rows1, bf16),
        *reduction(rows2, f32),
        dma,
        dma((2, nv)),
        dma((2, nv)),
        dma((2, ns, steps)),
        dma((total_steps,)),
        dma((ns, steps)),
        dma((8, most)),
        dma((8, most)),
    ]
    vmem = pl.BlockSpec(memory_space=pltpu.VMEM)
    smem = pl.BlockSpec(memory_space=pltpu.SMEM)
    hidden, grad_gcn, grad_gbias, grad_input, grad_recur, grad_bias = pl.pallas_call(
        functools.partial(kernel, sizes),
        out_shape=[
            jax.ShapeDtypeStruct((total_steps, rows, hid), bf16),
            jax.ShapeDtypeStruct((width, width), f32),
            jax.ShapeDtypeStruct((1, width), f32),
            jax.ShapeDtypeStruct((width, 4 * hid), f32),
            jax.ShapeDtypeStruct((hid, 4 * hid), f32),
            jax.ShapeDtypeStruct((1, 4 * hid), f32),
        ],
        in_specs=[vmem, smem, vmem, pl.BlockSpec(memory_space=pl.ANY)] + [vmem] * 6,
        out_specs=[vmem] * 6,
        scratch_shapes=scratch,
        compiler_params=pltpu.CompilerParams(
            collective_id=0, has_side_effects=True, vmem_limit_bytes=48 * 2**20
        ),
    )(
        request,
        places,
        features.reshape(steps, row_blocks, tile, width),
        tile_vals,
        gcn_weight,
        gcn_bias.reshape(1, -1),
        input_weight,
        recur_weight,
        lstm_bias.reshape(1, -1),
        jnp.transpose(hidden_grad[0], (1, 0, 2)),
    )
    hidden_states = jnp.transpose(hidden, (1, 0, 2))[None]
    return (
        hidden_states,
        grad_gcn,
        grad_gbias.reshape(-1),
        grad_input,
        grad_recur,
        grad_bias.reshape(-1),
    )


def solution(mesh):
    sizes = {axis: mesh.shape[axis] for axis in ("snap", "vtx")}
    return jax.shard_map(
        functools.partial(on_device, sizes),
        mesh=mesh,
        in_specs=(
            P("snap", "vtx", None),
            P("snap", "vtx", None, None, None),
            P("snap", "vtx", None),
            P("snap", "vtx"),
            P(),
            P(),
            P(),
            P(),
            P(),
            P("vtx", "snap", None, None),
        ),
        out_specs=(P("vtx", "snap", None, None), P(), P(), P(), P(), P()),
        check_vma=False,
    )
```

```python
import functools

import jax
import jax.numpy as jnp
from jax import lax
from jax.experimental import pallas as pl
from jax.experimental.pallas import tpu as pltpu
from jax.sharding import PartitionSpec as P

MESH = pl.DeviceIdType.MESH
LANES = 128


def sigmoid(x):
    return 0.5 * jnp.tanh(0.5 * x) + 0.5


class Reducer:
    def __init__(self, me, sizes, own, part_in, part_sum, chunk_in, whole, sems):
        self.me, self.sizes = me, sizes
        self.own, self.part_in, self.part_sum = own, part_in, part_sum
        self.chunk_in, self.whole, self.sems = chunk_in, whole, sems
        self.part = part_sum.shape[0]
        self.chunk = self.part // sizes["vtx"]

    def rows(self, snap, vtx=None):
        if vtx is None:
            return pl.ds(pl.multiple_of(snap * self.part, self.part), self.part)
        return pl.ds(pl.multiple_of(snap * self.part + vtx * self.chunk, self.chunk), self.chunk)

    def copy(self, stage, k, forward):
        axis = ("snap", "vtx", "vtx", "snap")[stage]
        n, me = self.sizes[axis], self.me[axis]
        peer = lax.rem(me + k, n) if forward else lax.rem(me - k + n, n)
        if stage == 0:
            src, dst = self.own.at[self.rows(peer)], self.part_in.at[k - 1]
        elif stage == 1:
            here = pl.ds(pl.multiple_of(peer * self.chunk, self.chunk), self.chunk)
            src, dst = self.part_sum.at[here], self.chunk_in.at[k - 1]
        elif stage == 2:
            src = dst = self.whole.at[self.rows(self.me["snap"], me if forward else peer)]
        else:
            src = dst = self.whole.at[self.rows(me if forward else peer)]
        return pltpu.make_async_remote_copy(
            src_ref=src,
            dst_ref=dst,
            send_sem=self.sems.at[2 * stage, k],
            recv_sem=self.sems.at[2 * stage + 1, k],
            device_id={axis: peer},
            device_id_type=MESH,
        )

    def peers(self, stage):
        return range(1, self.sizes[("snap", "vtx", "vtx", "snap")[stage]])

    def start(self, stage):
        for k in self.peers(stage):
            self.copy(stage, k, True).start()

    def finish(self, stage):
        for k in self.peers(stage):
            self.copy(stage, k, False).wait_recv()
        if stage == 0:
            total = self.own[self.rows(self.me["snap"]), :]
            for k in self.peers(stage):
                total = total + self.part_in[k - 1].astype(jnp.float32)
            self.part_sum[...] = total
        elif stage == 1:
            here = pl.ds(pl.multiple_of(self.me["vtx"] * self.chunk, self.chunk), self.chunk)
            total = self.part_sum[here, :]
            for k in self.peers(stage):
                total = total + self.chunk_in[k - 1].astype(jnp.float32)
            place = self.rows(self.me["snap"], self.me["vtx"])
            self.whole[place, :] = total.astype(self.whole.dtype)

    def drain(self):
        for stage in range(4):
            for k in self.peers(stage):
                self.copy(stage, k, True).wait_send()


def kernel(
    sizes,
    request_hbm,
    place_ref,
    feat_hbm,
    tiles_ref,
    gcn_w_hbm,
    gcn_b_hbm,
    in_w_hbm,
    rec_w_hbm,
    lstm_b_hbm,
    hgrad_hbm,
    hid_out,
    gcn_out,
    gcn_b_out,
    in_out,
    rec_out,
    lstm_b_out,
    tiles,
    request_ref,
    feat_ref,
    gcn_w_ref,
    gcn_b_ref,
    lstm_b_ref,
    hgrad_ref,
    asked,
    staged,
    fetched,
    aggregated,
    pre_act,
    layer,
    xs,
    hs,
    acts,
    cells,
    dlayer,
    dlayer_in,
    dcell,
    back,
    weights,
    weights_t,
    lstm_b_sum,
    sum1,
    part_in1,
    part1,
    chunk_in1,
    whole1,
    sum2,
    part_in2,
    part2,
    chunk_in2,
    whole2,
    load_sem,
    ask_sem,
    feat_sem,
    layer_sem,
    back_send,
    back_recv,
    sems1,
    sems2,
):
    ns, nv = sizes["snap"], sizes["vtx"]
    me_s, me_v = lax.axis_index("snap"), lax.axis_index("vtx")
    me = {"snap": me_s, "vtx": me_v}
    steps, verts, width = layer.shape
    _, row_blocks, slots, tile, _ = tiles_ref.shape
    total_steps, rows, hid = hgrad_ref.shape

    def remote(src, dst, send, recv, axis, peer):
        return pltpu.make_async_remote_copy(
            src_ref=src,
            dst_ref=dst,
            send_sem=send,
            recv_sem=recv,
            device_id={axis: peer},
            device_id_type=MESH,
        )

    barrier = pltpu.get_barrier_semaphore()
    for axis in ("snap", "vtx"):
        for k in range(1, sizes[axis]):
            peer = lax.rem(me[axis] + k, sizes[axis])
            pl.semaphore_signal(barrier, inc=1, device_id={axis: peer}, device_id_type=MESH)
    loads = [
        pltpu.make_async_copy(src, dst, load_sem.at[n])
        for n, (src, dst) in enumerate(
            [
                (request_hbm, request_ref),
                (feat_hbm, feat_ref),
                (tiles_ref, tiles),
                (in_w_hbm, weights.at[pl.ds(0, width)]),
                (rec_w_hbm, weights.at[pl.ds(width, hid)]),
                (gcn_w_hbm, gcn_w_ref),
                (gcn_b_hbm, gcn_b_ref),
                (lstm_b_hbm, lstm_b_ref),
                (hgrad_hbm, hgrad_ref),
            ]
        )
    ]
    for load in loads:
        load.start()
    for s in range(steps):
        fetched[s][nv] = jnp.zeros((tile, width), jnp.bfloat16)
    loads[0].wait()
    pl.semaphore_wait(barrier, ns + nv - 2)

    def ask(k, forward):
        peer = lax.rem(me_v + k, nv) if forward else lax.rem(me_v - k + nv, nv)
        return remote(
            request_ref.at[peer], asked.at[k], ask_sem.at[0, k], ask_sem.at[1, k], "vtx", peer
        )

    def give(k, s, forward):
        peer = lax.rem(me_v + k, nv) if forward else lax.rem(me_v - k + nv, nv)
        return remote(
            staged.at[k, s],
            fetched[s].at[me_v if forward else peer],
            feat_sem.at[0, k, s],
            feat_sem.at[1, k, s],
            "vtx",
            peer,
        )

    for k in range(1, nv):
        ask(k, True).start()
    loads[1].wait()
    for k in range(1, nv):
        ask(nv - k, False).wait_recv()
        wanted = asked[nv - k]
        staged[k, 0] = feat_ref[0, wanted[0, 0]]
        give(k, 0, True).start()
        for s in range(1, steps):
            staged[k, s] = feat_ref[s, wanted[s, 0]]
    own_request = request_ref[me_v]
    for s in range(steps):
        fetched[s][me_v] = feat_ref[s, own_request[s, 0]]
    for load in loads[2:]:
        load.wait()
    weights_t[...] = weights[...].T

    def give_next(s):
        for k in range(1, nv):
            give(k, s - 1, True).wait_send()
            give(k, s, True).start()

    if steps > 1:
        give_next(1)

    def layer_copy(k, s, forward):
        peer = lax.rem(me_s + k, ns) if forward else lax.rem(me_s - k + ns, ns)
        holder = me_s if forward else peer
        return remote(
            layer.at[s, pl.ds(pl.multiple_of(peer * rows, rows), rows)],
            xs.at[holder * steps + s],
            layer_sem.at[0, k, s],
            layer_sem.at[1, k, s],
            "snap",
            peer,
        )

    def convolve(s):
        for k in range(1, nv):
            give(k, s, False).wait_recv()
        if 0 < s < steps - 1:
            give_next(s + 1)
        for r in range(row_blocks):
            picked = [fetched[s][place_ref[s, r, m]] for m in range(slots)]
            left = jnp.concatenate([tiles[s, r, m] for m in range(slots)], axis=1)
            summed = jnp.dot(
                left, jnp.concatenate(picked, axis=0), preferred_element_type=jnp.float32
            )
            aggregated[s, pl.ds(r * tile, tile), :] = summed.astype(jnp.bfloat16)
        pre = (
            jnp.dot(aggregated[s], gcn_w_ref[...], preferred_element_type=jnp.float32)
            + gcn_b_ref[...]
        )
        pre_act[s] = pre
        layer[s] = (pre * sigmoid(pre)).astype(jnp.bfloat16)
        for k in range(1, ns):
            layer_copy(k, s, True).start()
        xs[me_s * steps + s] = layer[s, pl.ds(pl.multiple_of(me_s * rows, rows), rows), :]

    for s in range(steps):
        convolve(s)

    hs[0] = jnp.zeros((rows, hid), jnp.bfloat16)
    cells[0] = jnp.zeros((rows, hid), jnp.float32)

    def advance(t, carry):
        holder = lax.div(t, steps)

        @pl.when(holder != me_s)
        def _():
            k = lax.rem(me_s - holder + ns, ns)
            layer_copy(k, lax.rem(t, steps), False).wait_recv()

        both = jnp.concatenate([xs[t], hs[t]], axis=1)
        gates = jnp.dot(both, weights[...], preferred_element_type=jnp.float32) + lstm_b_ref[...]
        gate_in = sigmoid(gates[:, :hid])
        gate_keep = sigmoid(gates[:, hid : 2 * hid])
        gate_new = jnp.tanh(gates[:, 2 * hid : 3 * hid])
        gate_out = sigmoid(gates[:, 3 * hid :])
        cell = gate_keep * cells[t] + gate_in * gate_new
        out = (gate_out * jnp.tanh(cell)).astype(jnp.bfloat16)
        acts[t, 0] = gate_in
        acts[t, 1] = gate_keep
        acts[t, 2] = gate_new
        acts[t, 3] = gate_out
        cells[t + 1] = cell
        hs[t + 1] = out
        hid_out[t] = out
        return carry

    lax.fori_loop(0, total_steps, advance, 0)

    def back_copy(t, peer, forward):
        holder = lax.div(t, steps)
        s = lax.rem(t, steps)
        k = lax.rem(holder - me_s + ns, ns) if forward else lax.rem(me_s - peer + ns, ns)
        sender = me_s if forward else peer
        return remote(
            dlayer.at[t],
            dlayer_in.at[s, pl.ds(pl.multiple_of(sender * rows, rows), rows)],
            back_send.at[t],
            back_recv.at[k, s],
            "snap",
            holder if forward else peer,
        )

    dcell[...] = jnp.zeros((rows, hid), jnp.float32)
    back[...] = jnp.zeros((rows, hid), jnp.float32)
    lstm_b_sum[...] = jnp.zeros(lstm_b_sum.shape, jnp.float32)
    sum1[...] = jnp.zeros(sum1.shape, jnp.float32)
    height = width + hid

    def retreat(step, carry):
        t = total_steps - 1 - step
        gate_in, gate_keep, gate_new, gate_out = (acts[t, q] for q in range(4))
        squash = jnp.tanh(cells[t + 1])
        dh = hgrad_ref[t].astype(jnp.float32) + back[...]
        dc = dcell[...] + dh * gate_out * (1.0 - squash * squash)
        dgates = jnp.concatenate(
            [
                dc * gate_new * gate_in * (1.0 - gate_in),
                dc * cells[t] * gate_keep * (1.0 - gate_keep),
                dc * gate_in * (1.0 - gate_new * gate_new),
                dh * squash * gate_out * (1.0 - gate_out),
            ],
            axis=1,
        ).astype(jnp.bfloat16)
        dcell[...] = dc * gate_keep
        both_back = jnp.dot(dgates, weights_t[...], preferred_element_type=jnp.float32)
        back[...] = both_back[:, width:]
        grad = both_back[:, :width].astype(jnp.bfloat16)
        holder = lax.div(t, steps)

        @pl.when(holder != me_s)
        def _():
            dlayer[t] = grad
            back_copy(t, None, True).start()

        @pl.when(holder == me_s)
        def _():
            place = pl.ds(pl.multiple_of(me_s * rows, rows), rows)
            dlayer_in[lax.rem(t, steps), place, :] = grad

        lstm_b_sum[...] += jnp.sum(
            dgates.astype(jnp.float32).reshape(rows // 8, 8, 4 * hid), axis=0
        )
        both = jnp.concatenate([xs[t], hs[t]], axis=1)
        term = lax.dot_general(
            both, dgates, (((0,), (0,)), ((), ())), preferred_element_type=jnp.float32
        )
        for q in range(4):
            sum1[q * height : (q + 1) * height, :] += term[:, q * hid : (q + 1) * hid]
        return carry

    lax.fori_loop(0, total_steps, retreat, 0)

    first = Reducer(me, sizes, sum1, part_in1, part1, chunk_in1, whole1, sems1)
    second = Reducer(me, sizes, sum2, part_in2, part2, chunk_in2, whole2, sems2)
    first.start(0)

    sum2[...] = jnp.zeros(sum2.shape, jnp.float32)
    gcn_b_sum = jnp.zeros((1, width), jnp.float32)
    for s in reversed(range(steps)):
        for k in range(1, ns):
            src = lax.rem(me_s - k + ns, ns)
            back_copy(me_s * steps + s, src, False).wait_recv()
        pre = pre_act[s]
        slope = sigmoid(pre)
        dpre = (dlayer_in[s].astype(jnp.float32) * slope * (1.0 + pre * (1.0 - slope))).astype(
            jnp.bfloat16
        )
        sum2[:width, :] += lax.dot_general(
            aggregated[s], dpre, (((0,), (0,)), ((), ())), preferred_element_type=jnp.float32
        )
        gcn_b_sum = gcn_b_sum + jnp.sum(dpre.astype(jnp.float32), axis=0, keepdims=True)
    lstm_b = jnp.sum(lstm_b_sum[...], axis=0, keepdims=True)
    sum2[width : width + 1, :] = gcn_b_sum
    for q in range(4):
        sum2[width + 1 + q : width + 2 + q, :] = lstm_b[:, q * hid : (q + 1) * hid]

    second.start(0)
    for stage in range(4):
        first.finish(stage)
        if stage < 3:
            first.start(stage + 1)
        second.finish(stage)
        if stage < 3:
            second.start(stage + 1)

    for q in range(4):
        at = q * height
        span = slice(q * hid, (q + 1) * hid)
        in_out[:, span] = whole1[at : at + width, :].astype(jnp.float32)
        rec_out[:, span] = whole1[at + width : at + height, :].astype(jnp.float32)
        lstm_b_out[:, span] = whole2[width + 1 + q : width + 2 + q, :]
    gcn_out[...] = whole2[:width, :]
    gcn_b_out[...] = whole2[width : width + 1, :]

    for k in range(1, nv):
        ask(k, True).wait_send()
        give(k, steps - 1, True).wait_send()
    for k in range(1, ns):
        for s in range(steps):
            layer_copy(k, s, True).wait_send()

    def drain(t, carry):
        @pl.when(lax.div(t, steps) != me_s)
        def _():
            back_copy(t, None, True).wait_send()

        return carry

    lax.fori_loop(0, total_steps, drain, 0)
    first.drain()
    second.drain()


def write_out(*refs):
    *arrays, sems = refs
    half = len(arrays) // 2
    copies = [
        pltpu.make_async_copy(src, dst, sems.at[n])
        for n, (src, dst) in enumerate(zip(arrays[:half], arrays[half:]))
    ]
    for copy in copies:
        copy.start()
    for copy in copies:
        copy.wait()


def on_device(
    sizes,
    features,
    tile_vals,
    tile_cols,
    tile_count,
    gcn_weight,
    gcn_bias,
    input_weight,
    recur_weight,
    lstm_bias,
    hidden_grad,
):
    ns, nv = sizes["snap"], sizes["vtx"]
    steps, verts, width = features.shape
    _, row_blocks, slots, tile, _ = tile_vals.shape
    hid = recur_weight.shape[0]
    _, rows, total_steps, _ = hidden_grad.shape
    bf16, f32 = jnp.bfloat16, jnp.float32

    blocks = tile_cols[None]
    low = lax.broadcasted_iota(jnp.int32, (nv,) + tile_cols.shape, 0) * row_blocks
    named = jnp.where((blocks >= low) & (blocks < low + row_blocks), blocks - low, 0)
    request = jnp.max(named, axis=(2, 3))
    request = jnp.pad(request, ((0, 0), (0, -steps % 8)))
    request = jnp.broadcast_to(request[:, :, None], request.shape + (LANES,))

    live = lax.broadcasted_iota(jnp.int32, tile_cols.shape, 2) < tile_count[:, :, None]
    places = jnp.where(live, tile_cols // row_blocks, nv)

    def padded(count, unit):
        unit = unit * ns * nv
        return -(-count // unit) * unit

    rows1 = padded(4 * (width + hid), 16)
    rows2 = padded(width + 5, 8)
    most = max(ns, nv)
    dma = pltpu.SemaphoreType.DMA

    def reduction(count, kept):
        part = count // ns
        return [
            pltpu.VMEM((count, LANES), f32),
            pltpu.VMEM((ns - 1, part, LANES), f32),
            pltpu.VMEM((part, LANES), f32),
            pltpu.VMEM((nv - 1, part // nv, LANES), f32),
            pltpu.VMEM((count, LANES), kept),
        ]

    scratch = [
        pltpu.VMEM(tile_vals.shape, bf16),
        pltpu.VMEM(request.shape, jnp.int32),
        pltpu.VMEM((steps, row_blocks, tile, width), bf16),
        pltpu.VMEM(gcn_weight.shape, bf16),
        pltpu.VMEM((1, width), f32),
        pltpu.VMEM((1, 4 * hid), f32),
        pltpu.VMEM((total_steps, rows, hid), bf16),
        pltpu.VMEM((nv,) + request.shape[1:], jnp.int32),
        pltpu.VMEM((nv, steps, tile, width), bf16),
        [pltpu.VMEM((nv + 1, tile, width), bf16) for _ in range(steps)],
        pltpu.VMEM((steps, verts, width), bf16),
        pltpu.VMEM((steps, verts, width), f32),
        pltpu.VMEM((steps, verts, width), bf16),
        pltpu.VMEM((total_steps, rows, width), bf16),
        pltpu.VMEM((total_steps + 1, rows, hid), bf16),
        pltpu.VMEM((total_steps, 4, rows, hid), f32),
        pltpu.VMEM((total_steps + 1, rows, hid), f32),
        pltpu.VMEM((total_steps, rows, width), bf16),
        pltpu.VMEM((steps, verts, width), bf16),
        pltpu.VMEM((rows, hid), f32),
        pltpu.VMEM((rows, hid), f32),
        pltpu.VMEM((width + hid, 4 * hid), bf16),
        pltpu.VMEM((4 * hid, width + hid), bf16),
        pltpu.VMEM((8, 4 * hid), f32),
        *reduction(rows1, bf16),
        *reduction(rows2, f32),
        dma((9,)),
        dma((2, nv)),
        dma((2, nv, steps)),
        dma((2, ns, steps)),
        dma((total_steps,)),
        dma((ns, steps)),
        dma((8, most)),
        dma((8, most)),
    ]
    vmem = pl.BlockSpec(memory_space=pltpu.VMEM)
    smem = pl.BlockSpec(memory_space=pltpu.SMEM)
    hbm = pl.BlockSpec(memory_space=pl.ANY)
    hidden, *grads = pl.pallas_call(
        functools.partial(kernel, sizes),
        out_shape=[
            jax.ShapeDtypeStruct((total_steps, rows, hid), bf16),
            jax.ShapeDtypeStruct((width, width), f32),
            jax.ShapeDtypeStruct((1, width), f32),
            jax.ShapeDtypeStruct((width, 4 * hid), f32),
            jax.ShapeDtypeStruct((hid, 4 * hid), f32),
            jax.ShapeDtypeStruct((1, 4 * hid), f32),
        ],
        in_specs=[hbm, smem] + [hbm] * 8,
        out_specs=[vmem] * 6,
        scratch_shapes=scratch,
        compiler_params=pltpu.CompilerParams(
            collective_id=0, has_side_effects=True, vmem_limit_bytes=60 * 2**20
        ),
    )(
        request,
        places,
        features.reshape(steps, row_blocks, tile, width),
        tile_vals,
        gcn_weight,
        gcn_bias.reshape(1, -1),
        input_weight,
        recur_weight,
        lstm_bias.reshape(1, -1),
        jnp.transpose(hidden_grad[0], (1, 0, 2)),
    )
    grad_gcn, grad_gbias, grad_input, grad_recur, grad_bias = pl.pallas_call(
        write_out,
        out_shape=[jax.ShapeDtypeStruct(grad.shape, f32) for grad in grads],
        in_specs=[hbm] * len(grads),
        out_specs=[hbm] * len(grads),
        scratch_shapes=[dma((len(grads),))],
    )(*grads)
    hidden_states = jnp.transpose(hidden, (1, 0, 2))[None]
    return (
        hidden_states,
        grad_gcn,
        grad_gbias.reshape(-1),
        grad_input,
        grad_recur,
        grad_bias.reshape(-1),
    )


def solution(mesh):
    sizes = {axis: mesh.shape[axis] for axis in ("snap", "vtx")}
    return jax.shard_map(
        functools.partial(on_device, sizes),
        mesh=mesh,
        in_specs=(
            P("snap", "vtx", None),
            P("snap", "vtx", None, None, None),
            P("snap", "vtx", None),
            P("snap", "vtx"),
            P(),
            P(),
            P(),
            P(),
            P(),
            P("vtx", "snap", None, None),
        ),
        out_specs=(P("vtx", "snap", None, None), P(), P(), P(), P(), P()),
        check_vma=False,
    )
```

```python
import functools

import jax
import jax.numpy as jnp
from jax import lax
from jax.experimental import pallas as pl
from jax.experimental.pallas import tpu as pltpu
from jax.sharding import PartitionSpec as P

MESH = pl.DeviceIdType.MESH
LANES = 128


def sigmoid(x):
    return 0.5 * jnp.tanh(0.5 * x) + 0.5


class Reducer:
    def __init__(self, me, sizes, own, sent, part_in, part_sum, part_sent, chunk_in, whole, sems):
        self.me, self.sizes = me, sizes
        self.own, self.sent, self.part_in = own, sent, part_in
        self.part_sum, self.part_sent = part_sum, part_sent
        self.chunk_in, self.whole, self.sems = chunk_in, whole, sems
        self.part = part_sum.shape[0]
        self.chunk = self.part // sizes["vtx"]

    def rows(self, snap, vtx=None):
        if vtx is None:
            return pl.ds(pl.multiple_of(snap * self.part, self.part), self.part)
        return pl.ds(pl.multiple_of(snap * self.part + vtx * self.chunk, self.chunk), self.chunk)

    def copy(self, stage, k, forward):
        axis = ("snap", "vtx", "vtx", "snap")[stage]
        n, me = self.sizes[axis], self.me[axis]
        peer = lax.rem(me + k, n) if forward else lax.rem(me - k + n, n)
        if stage == 0:
            src, dst = self.sent.at[self.rows(peer)], self.part_in.at[k - 1]
        elif stage == 1:
            here = pl.ds(pl.multiple_of(peer * self.chunk, self.chunk), self.chunk)
            src, dst = self.part_sent.at[here], self.chunk_in.at[k - 1]
        elif stage == 2:
            src = dst = self.whole.at[self.rows(self.me["snap"], me if forward else peer)]
        else:
            src = dst = self.whole.at[self.rows(me if forward else peer)]
        return pltpu.make_async_remote_copy(
            src_ref=src,
            dst_ref=dst,
            send_sem=self.sems.at[2 * stage, k],
            recv_sem=self.sems.at[2 * stage + 1, k],
            device_id={axis: peer},
            device_id_type=MESH,
        )

    def peers(self, stage):
        return range(1, self.sizes[("snap", "vtx", "vtx", "snap")[stage]])

    def start(self, stage):
        for k in self.peers(stage):
            self.copy(stage, k, True).start()

    def finish(self, stage):
        for k in self.peers(stage):
            self.copy(stage, k, False).wait_recv()
        if stage == 0:
            total = self.own[self.rows(self.me["snap"]), :]
            for k in self.peers(stage):
                total = total + self.part_in[k - 1].astype(jnp.float32)
            self.part_sum[...] = total
            if self.part_sent is not self.part_sum:
                self.part_sent[...] = total.astype(self.part_sent.dtype)
        elif stage == 1:
            here = pl.ds(pl.multiple_of(self.me["vtx"] * self.chunk, self.chunk), self.chunk)
            total = self.part_sum[here, :]
            for k in self.peers(stage):
                total = total + self.chunk_in[k - 1].astype(jnp.float32)
            place = self.rows(self.me["snap"], self.me["vtx"])
            self.whole[place, :] = total.astype(self.whole.dtype)

    def drain(self):
        for stage in range(4):
            for k in self.peers(stage):
                self.copy(stage, k, True).wait_send()


def kernel(
    sizes,
    cols_hbm,
    place_ref,
    feat_hbm,
    tiles_ref,
    gcn_w_hbm,
    gcn_b_hbm,
    in_w_hbm,
    rec_w_hbm,
    lstm_b_hbm,
    hgrad_hbm,
    hid_out,
    gcn_out,
    gcn_b_out,
    in_out,
    rec_out,
    lstm_b_out,
    tiles,
    cols_ref,
    request_ref,
    feat_ref,
    gcn_w_ref,
    gcn_b_ref,
    lstm_b_ref,
    hgrad_ref,
    hgrad,
    asked,
    staged,
    fetched,
    aggregated,
    pre_act,
    layer,
    xs,
    hs,
    acts,
    cells,
    dlayer,
    dlayer_in,
    dcell,
    back,
    weights,
    weights_t,
    lstm_b_sum,
    sum1,
    part_in1,
    part1,
    chunk_in1,
    whole1,
    sent1,
    part_sent1,
    sum2,
    part_in2,
    part2,
    chunk_in2,
    whole2,
    load_sem,
    ask_sem,
    feat_sem,
    layer_sem,
    back_send,
    back_recv,
    sems1,
    sems2,
):
    ns, nv = sizes["snap"], sizes["vtx"]
    me_s, me_v = lax.axis_index("snap"), lax.axis_index("vtx")
    me = {"snap": me_s, "vtx": me_v}
    steps, verts, width = layer.shape
    _, row_blocks, slots, tile, _ = tiles_ref.shape
    rows, total_steps, hid = hgrad_ref.shape

    def remote(src, dst, send, recv, axis, peer):
        return pltpu.make_async_remote_copy(
            src_ref=src,
            dst_ref=dst,
            send_sem=send,
            recv_sem=recv,
            device_id={axis: peer},
            device_id_type=MESH,
        )

    barrier = pltpu.get_barrier_semaphore()
    for axis in ("snap", "vtx"):
        for k in range(1, sizes[axis]):
            peer = lax.rem(me[axis] + k, sizes[axis])
            pl.semaphore_signal(barrier, inc=1, device_id={axis: peer}, device_id_type=MESH)
    loads = [
        pltpu.make_async_copy(src, dst, load_sem.at[n])
        for n, (src, dst) in enumerate(
            [
                (cols_hbm, cols_ref),
                (feat_hbm, feat_ref),
                (tiles_ref, tiles),
                (in_w_hbm, weights.at[pl.ds(0, width)]),
                (rec_w_hbm, weights.at[pl.ds(width, hid)]),
                (gcn_w_hbm, gcn_w_ref),
                (gcn_b_hbm, gcn_b_ref),
                (lstm_b_hbm, lstm_b_ref),
                (hgrad_hbm.at[0], hgrad_ref),
            ]
        )
    ]
    for load in loads:
        load.start()
    for s in range(steps):
        fetched[s][nv] = jnp.zeros((tile, width), jnp.bfloat16)
    loads[0].wait()
    for p in range(nv):
        blocks = cols_ref[...] - p * row_blocks
        named = jnp.where((blocks >= 0) & (blocks < row_blocks), blocks, 0)
        for s in range(steps):
            block = jnp.max(named[s], axis=(0, 1), keepdims=True)
            request_ref[p, s] = jnp.broadcast_to(block, (8, LANES))
    pl.semaphore_wait(barrier, ns + nv - 2)

    def ask(k, forward):
        peer = lax.rem(me_v + k, nv) if forward else lax.rem(me_v - k + nv, nv)
        return remote(
            request_ref.at[peer], asked.at[k], ask_sem.at[0, k], ask_sem.at[1, k], "vtx", peer
        )

    def give(k, s, forward):
        peer = lax.rem(me_v + k, nv) if forward else lax.rem(me_v - k + nv, nv)
        return remote(
            staged.at[k, s],
            fetched[s].at[me_v if forward else peer],
            feat_sem.at[0, k, s],
            feat_sem.at[1, k, s],
            "vtx",
            peer,
        )

    for k in range(1, nv):
        ask(k, True).start()
    loads[1].wait()
    for k in range(1, nv):
        ask(nv - k, False).wait_recv()
        wanted = asked[nv - k]
        staged[k, 0] = feat_ref[0, wanted[0, 0, 0]]
        give(k, 0, True).start()
        for s in range(1, steps):
            staged[k, s] = feat_ref[s, wanted[s, 0, 0]]
    own_request = request_ref[me_v]
    for s in range(steps):
        fetched[s][me_v] = feat_ref[s, own_request[s, 0, 0]]
    for load in loads[2:]:
        load.wait()
    weights_t[...] = weights[...].T

    def give_next(s):
        for k in range(1, nv):
            give(k, s - 1, True).wait_send()
            give(k, s, True).start()

    if steps > 1:
        give_next(1)
    hgrad[...] = hgrad_ref[...].astype(jnp.float32).reshape(rows * total_steps, hid)

    def layer_copy(k, s, forward):
        peer = lax.rem(me_s + k, ns) if forward else lax.rem(me_s - k + ns, ns)
        holder = me_s if forward else peer
        return remote(
            layer.at[s, pl.ds(pl.multiple_of(peer * rows, rows), rows)],
            xs.at[holder * steps + s],
            layer_sem.at[0, k, s],
            layer_sem.at[1, k, s],
            "snap",
            peer,
        )

    def convolve(s):
        for k in range(1, nv):
            give(k, s, False).wait_recv()
        if 0 < s < steps - 1:
            give_next(s + 1)
        for r in range(row_blocks):
            picked = [fetched[s][place_ref[s, r, m]] for m in range(slots)]
            left = jnp.concatenate([tiles[s, r, m] for m in range(slots)], axis=1)
            summed = jnp.dot(
                left, jnp.concatenate(picked, axis=0), preferred_element_type=jnp.float32
            )
            aggregated[s, pl.ds(r * tile, tile), :] = summed.astype(jnp.bfloat16)
        pre = (
            jnp.dot(aggregated[s], gcn_w_ref[...], preferred_element_type=jnp.float32)
            + gcn_b_ref[...]
        )
        pre_act[s] = pre
        layer[s] = (pre * sigmoid(pre)).astype(jnp.bfloat16)
        for k in range(1, ns):
            layer_copy(k, s, True).start()
        xs[me_s * steps + s] = layer[s, pl.ds(pl.multiple_of(me_s * rows, rows), rows), :]

    for s in range(steps):
        convolve(s)

    hs[0] = jnp.zeros((rows, hid), jnp.bfloat16)
    cells[0] = jnp.zeros((rows, hid), jnp.float32)

    def advance(t, carry):
        holder = lax.div(t, steps)

        @pl.when(holder != me_s)
        def _():
            k = lax.rem(me_s - holder + ns, ns)
            layer_copy(k, lax.rem(t, steps), False).wait_recv()

        both = jnp.concatenate([xs[t], hs[t]], axis=1)
        gates = jnp.dot(both, weights[...], preferred_element_type=jnp.float32) + lstm_b_ref[...]
        gate_in = sigmoid(gates[:, :hid])
        gate_keep = sigmoid(gates[:, hid : 2 * hid])
        gate_new = jnp.tanh(gates[:, 2 * hid : 3 * hid])
        gate_out = sigmoid(gates[:, 3 * hid :])
        cell = gate_keep * cells[t] + gate_in * gate_new
        out = (gate_out * jnp.tanh(cell)).astype(jnp.bfloat16)
        acts[t, 0] = gate_in
        acts[t, 1] = gate_keep
        acts[t, 2] = gate_new
        acts[t, 3] = gate_out
        cells[t + 1] = cell
        hs[t + 1] = out
        hid_out[t] = out
        return carry

    lax.fori_loop(0, total_steps, advance, 0)

    def back_copy(t, peer, forward):
        holder = lax.div(t, steps)
        s = lax.rem(t, steps)
        k = lax.rem(holder - me_s + ns, ns) if forward else lax.rem(me_s - peer + ns, ns)
        sender = me_s if forward else peer
        return remote(
            dlayer.at[t],
            dlayer_in.at[s, pl.ds(pl.multiple_of(sender * rows, rows), rows)],
            back_send.at[t],
            back_recv.at[k, s],
            "snap",
            holder if forward else peer,
        )

    dcell[...] = jnp.zeros((rows, hid), jnp.float32)
    back[...] = jnp.zeros((rows, hid), jnp.float32)
    lstm_b_sum[...] = jnp.zeros(lstm_b_sum.shape, jnp.float32)
    sum1[...] = jnp.zeros(sum1.shape, jnp.float32)
    height = width + hid

    def retreat(step, carry):
        t = total_steps - 1 - step
        gate_in, gate_keep, gate_new, gate_out = (acts[t, q] for q in range(4))
        squash = jnp.tanh(cells[t + 1])
        dh = hgrad[pl.ds(t, rows, stride=total_steps), :] + back[...]
        dc = dcell[...] + dh * gate_out * (1.0 - squash * squash)
        dgates = jnp.concatenate(
            [
                dc * gate_new * gate_in * (1.0 - gate_in),
                dc * cells[t] * gate_keep * (1.0 - gate_keep),
                dc * gate_in * (1.0 - gate_new * gate_new),
                dh * squash * gate_out * (1.0 - gate_out),
            ],
            axis=1,
        ).astype(jnp.bfloat16)
        dcell[...] = dc * gate_keep
        both_back = jnp.dot(dgates, weights_t[...], preferred_element_type=jnp.float32)
        back[...] = both_back[:, width:]
        grad = both_back[:, :width].astype(jnp.bfloat16)
        holder = lax.div(t, steps)

        @pl.when(holder != me_s)
        def _():
            dlayer[t] = grad
            back_copy(t, None, True).start()

        @pl.when(holder == me_s)
        def _():
            place = pl.ds(pl.multiple_of(me_s * rows, rows), rows)
            dlayer_in[lax.rem(t, steps), place, :] = grad

        lstm_b_sum[...] += jnp.sum(
            dgates.astype(jnp.float32).reshape(rows // 8, 8, 4 * hid), axis=0
        )
        both = jnp.concatenate([xs[t], hs[t]], axis=1)
        term = lax.dot_general(
            both, dgates, (((0,), (0,)), ((), ())), preferred_element_type=jnp.float32
        )
        for q in range(4):
            sum1[q * height : (q + 1) * height, :] += term[:, q * hid : (q + 1) * hid]
        return carry

    lax.fori_loop(0, total_steps, retreat, 0)

    first = Reducer(
        me, sizes, sum1, sent1, part_in1, part1, part_sent1, chunk_in1, whole1, sems1
    )
    second = Reducer(
        me, sizes, sum2, sum2, part_in2, part2, part2, chunk_in2, whole2, sems2
    )
    sent1[...] = sum1[...].astype(jnp.bfloat16)
    first.start(0)

    sum2[...] = jnp.zeros(sum2.shape, jnp.float32)
    gcn_b_sum = jnp.zeros((1, width), jnp.float32)
    for s in reversed(range(steps)):
        for k in range(1, ns):
            src = lax.rem(me_s - k + ns, ns)
            back_copy(me_s * steps + s, src, False).wait_recv()
        pre = pre_act[s]
        slope = sigmoid(pre)
        dpre = (dlayer_in[s].astype(jnp.float32) * slope * (1.0 + pre * (1.0 - slope))).astype(
            jnp.bfloat16
        )
        sum2[:width, :] += lax.dot_general(
            aggregated[s], dpre, (((0,), (0,)), ((), ())), preferred_element_type=jnp.float32
        )
        gcn_b_sum = gcn_b_sum + jnp.sum(dpre.astype(jnp.float32), axis=0, keepdims=True)
    lstm_b = jnp.sum(lstm_b_sum[...], axis=0, keepdims=True)
    sum2[width : width + 1, :] = gcn_b_sum
    for q in range(4):
        sum2[width + 1 + q : width + 2 + q, :] = lstm_b[:, q * hid : (q + 1) * hid]

    second.start(0)
    for stage in range(4):
        first.finish(stage)
        if stage < 3:
            first.start(stage + 1)
        second.finish(stage)
        if stage < 3:
            second.start(stage + 1)

    for q in range(4):
        at = q * height
        span = slice(q * hid, (q + 1) * hid)
        in_out[:, span] = whole1[at : at + width, :].astype(jnp.float32)
        rec_out[:, span] = whole1[at + width : at + height, :].astype(jnp.float32)
        lstm_b_out[:, span] = whole2[width + 1 + q : width + 2 + q, :]
    gcn_out[...] = whole2[:width, :]
    gcn_b_out[...] = whole2[width : width + 1, :]

    for k in range(1, nv):
        ask(k, True).wait_send()
        give(k, steps - 1, True).wait_send()
    for k in range(1, ns):
        for s in range(steps):
            layer_copy(k, s, True).wait_send()

    def drain(t, carry):
        @pl.when(lax.div(t, steps) != me_s)
        def _():
            back_copy(t, None, True).wait_send()

        return carry

    lax.fori_loop(0, total_steps, drain, 0)
    first.drain()
    second.drain()


def write_out(*refs):
    *arrays, sems = refs
    n = len(arrays) // 3
    srcs, dsts, held = arrays[:n], arrays[n : 2 * n], arrays[2 * n :]
    ins = [pltpu.make_async_copy(srcs[i], held[i], sems.at[0, i]) for i in range(n)]
    outs = [pltpu.make_async_copy(held[i], dsts[i], sems.at[1, i]) for i in range(n)]
    for copy in ins:
        copy.start()
    for copy_in, copy_out in zip(ins, outs):
        copy_in.wait()
        copy_out.start()
    for copy in outs:
        copy.wait()


def on_device(
    sizes,
    features,
    tile_vals,
    tile_cols,
    tile_count,
    gcn_weight,
    gcn_bias,
    input_weight,
    recur_weight,
    lstm_bias,
    hidden_grad,
):
    ns, nv = sizes["snap"], sizes["vtx"]
    steps, verts, width = features.shape
    _, row_blocks, slots, tile, _ = tile_vals.shape
    hid = recur_weight.shape[0]
    _, rows, total_steps, _ = hidden_grad.shape
    bf16, f32 = jnp.bfloat16, jnp.float32

    live = lax.broadcasted_iota(jnp.int32, tile_cols.shape, 2) < tile_count[:, :, None]
    places = jnp.where(live, tile_cols // row_blocks, nv)

    def padded(count, unit):
        unit = unit * ns * nv
        return -(-count // unit) * unit

    rows1 = padded(4 * (width + hid), 16)
    rows2 = padded(width + 5, 8)
    most = max(ns, nv)
    dma = pltpu.SemaphoreType.DMA

    def reduction(count, kept):
        part = count // ns
        return [
            pltpu.VMEM((count, LANES), f32),
            pltpu.VMEM((ns - 1, part, LANES), kept),
            pltpu.VMEM((part, LANES), f32),
            pltpu.VMEM((nv - 1, part // nv, LANES), kept),
            pltpu.VMEM((count, LANES), kept),
        ]

    scratch = [
        pltpu.VMEM(tile_vals.shape, bf16),
        pltpu.VMEM(tile_cols.shape, jnp.int32),
        pltpu.VMEM((nv, steps, 8, LANES), jnp.int32),
        pltpu.VMEM((steps, row_blocks, tile, width), bf16),
        pltpu.VMEM(gcn_weight.shape, bf16),
        pltpu.VMEM((1, width), f32),
        pltpu.VMEM((1, 4 * hid), f32),
        pltpu.VMEM((rows, total_steps, hid), bf16),
        pltpu.VMEM((rows * total_steps, hid), f32),
        pltpu.VMEM((nv, steps, 8, LANES), jnp.int32),
        pltpu.VMEM((nv, steps, tile, width), bf16),
        [pltpu.VMEM((nv + 1, tile, width), bf16) for _ in range(steps)],
        pltpu.VMEM((steps, verts, width), bf16),
        pltpu.VMEM((steps, verts, width), f32),
        pltpu.VMEM((steps, verts, width), bf16),
        pltpu.VMEM((total_steps, rows, width), bf16),
        pltpu.VMEM((total_steps + 1, rows, hid), bf16),
        pltpu.VMEM((total_steps, 4, rows, hid), f32),
        pltpu.VMEM((total_steps + 1, rows, hid), f32),
        pltpu.VMEM((total_steps, rows, width), bf16),
        pltpu.VMEM((steps, verts, width), bf16),
        pltpu.VMEM((rows, hid), f32),
        pltpu.VMEM((rows, hid), f32),
        pltpu.VMEM((width + hid, 4 * hid), bf16),
        pltpu.VMEM((4 * hid, width + hid), bf16),
        pltpu.VMEM((8, 4 * hid), f32),
        *reduction(rows1, bf16),
        pltpu.VMEM((rows1, LANES), bf16),
        pltpu.VMEM((rows1 // ns, LANES), bf16),
        *reduction(rows2, f32),
        dma((9,)),
        dma((2, nv)),
        dma((2, nv, steps)),
        dma((2, ns, steps)),
        dma((total_steps,)),
        dma((ns, steps)),
        dma((8, most)),
        dma((8, most)),
    ]
    vmem = pl.BlockSpec(memory_space=pltpu.VMEM)
    smem = pl.BlockSpec(memory_space=pltpu.SMEM)
    hbm = pl.BlockSpec(memory_space=pl.ANY)
    hidden, *grads = pl.pallas_call(
        functools.partial(kernel, sizes),
        out_shape=[
            jax.ShapeDtypeStruct((total_steps, rows, hid), bf16),
            jax.ShapeDtypeStruct((width, width), f32),
            jax.ShapeDtypeStruct((1, width), f32),
            jax.ShapeDtypeStruct((width, 4 * hid), f32),
            jax.ShapeDtypeStruct((hid, 4 * hid), f32),
            jax.ShapeDtypeStruct((1, 4 * hid), f32),
        ],
        in_specs=[hbm, smem] + [hbm] * 8,
        out_specs=[vmem] * 6,
        scratch_shapes=scratch,
        compiler_params=pltpu.CompilerParams(
            collective_id=0, has_side_effects=True, vmem_limit_bytes=60 * 2**20
        ),
    )(
        tile_cols,
        places,
        features.reshape(steps, row_blocks, tile, width),
        tile_vals,
        gcn_weight,
        gcn_bias.reshape(1, -1),
        input_weight,
        recur_weight,
        lstm_bias.reshape(1, -1),
        hidden_grad,
    )
    grad_gcn, grad_gbias, grad_input, grad_recur, grad_bias = pl.pallas_call(
        write_out,
        out_shape=[jax.ShapeDtypeStruct(grad.shape, f32) for grad in grads],
        in_specs=[hbm] * len(grads),
        out_specs=[hbm] * len(grads),
        scratch_shapes=[pltpu.VMEM(grad.shape, f32) for grad in grads] + [dma((2, len(grads)))],
        compiler_params=pltpu.CompilerParams(vmem_limit_bytes=60 * 2**20),
    )(*grads)
    hidden_states = jnp.transpose(hidden, (1, 0, 2))[None]
    return (
        hidden_states,
        grad_gcn,
        grad_gbias.reshape(-1),
        grad_input,
        grad_recur,
        grad_bias.reshape(-1),
    )


def solution(mesh):
    sizes = {axis: mesh.shape[axis] for axis in ("snap", "vtx")}
    return jax.shard_map(
        functools.partial(on_device, sizes),
        mesh=mesh,
        in_specs=(
            P("snap", "vtx", None),
            P("snap", "vtx", None, None, None),
            P("snap", "vtx", None),
            P("snap", "vtx"),
            P(),
            P(),
            P(),
            P(),
            P(),
            P("vtx", "snap", None, None),
        ),
        out_specs=(P("vtx", "snap", None, None), P(), P(), P(), P(), P()),
        check_vma=False,
    )
```

```python
import functools

import jax
import jax.numpy as jnp
from jax import lax
from jax.experimental import pallas as pl
from jax.experimental.pallas import tpu as pltpu
from jax.sharding import PartitionSpec as P

MESH = pl.DeviceIdType.MESH
LANES = 128


def sigmoid(x):
    return 0.5 * jnp.tanh(0.5 * x) + 0.5


class Reducer:
    def __init__(self, me, sizes, own, sent, part_in, part_sum, part_sent, chunk_in, whole, sems):
        self.me, self.sizes = me, sizes
        self.own, self.sent, self.part_in = own, sent, part_in
        self.part_sum, self.part_sent = part_sum, part_sent
        self.chunk_in, self.whole, self.sems = chunk_in, whole, sems
        self.part = part_sum.shape[0]
        self.chunk = self.part // sizes["vtx"]

    def rows(self, snap, vtx=None):
        if vtx is None:
            return pl.ds(pl.multiple_of(snap * self.part, self.part), self.part)
        return pl.ds(pl.multiple_of(snap * self.part + vtx * self.chunk, self.chunk), self.chunk)

    def copy(self, stage, k, forward):
        axis = ("snap", "vtx", "vtx", "snap")[stage]
        n, me = self.sizes[axis], self.me[axis]
        peer = lax.rem(me + k, n) if forward else lax.rem(me - k + n, n)
        if stage == 0:
            src, dst = self.sent.at[self.rows(peer)], self.part_in.at[k - 1]
        elif stage == 1:
            here = pl.ds(pl.multiple_of(peer * self.chunk, self.chunk), self.chunk)
            src, dst = self.part_sent.at[here], self.chunk_in.at[k - 1]
        elif stage == 2:
            src = dst = self.whole.at[self.rows(self.me["snap"], me if forward else peer)]
        else:
            src = dst = self.whole.at[self.rows(me if forward else peer)]
        return pltpu.make_async_remote_copy(
            src_ref=src,
            dst_ref=dst,
            send_sem=self.sems.at[2 * stage, k],
            recv_sem=self.sems.at[2 * stage + 1, k],
            device_id={axis: peer},
            device_id_type=MESH,
        )

    def peers(self, stage):
        return range(1, self.sizes[("snap", "vtx", "vtx", "snap")[stage]])

    def start(self, stage):
        for k in self.peers(stage):
            self.copy(stage, k, True).start()

    def finish(self, stage):
        for k in self.peers(stage):
            self.copy(stage, k, False).wait_recv()
        if stage == 0:
            total = self.own[self.rows(self.me["snap"]), :]
            for k in self.peers(stage):
                total = total + self.part_in[k - 1].astype(jnp.float32)
            self.part_sum[...] = total
            if self.part_sent is not self.part_sum:
                self.part_sent[...] = total.astype(self.part_sent.dtype)
        elif stage == 1:
            here = pl.ds(pl.multiple_of(self.me["vtx"] * self.chunk, self.chunk), self.chunk)
            total = self.part_sum[here, :]
            for k in self.peers(stage):
                total = total + self.chunk_in[k - 1].astype(jnp.float32)
            place = self.rows(self.me["snap"], self.me["vtx"])
            self.whole[place, :] = total.astype(self.whole.dtype)

    def drain(self):
        for stage in range(4):
            for k in self.peers(stage):
                self.copy(stage, k, True).wait_send()


def kernel(
    sizes,
    cols_hbm,
    place_ref,
    feat_hbm,
    tiles_ref,
    gcn_w_hbm,
    gcn_b_hbm,
    in_w_hbm,
    rec_w_hbm,
    lstm_b_hbm,
    hgrad_hbm,
    hid_out,
    gcn_out,
    gcn_b_out,
    in_out,
    rec_out,
    lstm_b_out,
    tiles,
    cols_ref,
    request_ref,
    feat_ref,
    gcn_w_ref,
    gcn_b_ref,
    lstm_b_ref,
    hgrad_ref,
    hgrad,
    hidden,
    asked,
    staged,
    fetched,
    aggregated,
    pre_act,
    layer,
    xs,
    hs,
    acts,
    cells,
    dlayer,
    dlayer_in,
    dcell,
    back,
    weights,
    weights_t,
    lstm_b_sum,
    sum1,
    part_in1,
    part1,
    chunk_in1,
    whole1,
    sent1,
    part_sent1,
    sum2,
    part_in2,
    part2,
    chunk_in2,
    whole2,
    load_sem,
    ask_sem,
    feat_sem,
    layer_sem,
    back_send,
    back_recv,
    sems1,
    sems2,
):
    ns, nv = sizes["snap"], sizes["vtx"]
    me_s, me_v = lax.axis_index("snap"), lax.axis_index("vtx")
    me = {"snap": me_s, "vtx": me_v}
    steps, verts, width = layer.shape
    _, row_blocks, slots, tile, _ = tiles_ref.shape
    rows, total_steps, hid = hgrad_ref.shape

    def remote(src, dst, send, recv, axis, peer):
        return pltpu.make_async_remote_copy(
            src_ref=src,
            dst_ref=dst,
            send_sem=send,
            recv_sem=recv,
            device_id={axis: peer},
            device_id_type=MESH,
        )

    barrier = pltpu.get_barrier_semaphore()
    for axis in ("snap", "vtx"):
        for k in range(1, sizes[axis]):
            peer = lax.rem(me[axis] + k, sizes[axis])
            pl.semaphore_signal(barrier, inc=1, device_id={axis: peer}, device_id_type=MESH)
    loads = [
        pltpu.make_async_copy(src, dst, load_sem.at[n])
        for n, (src, dst) in enumerate(
            [
                (cols_hbm, cols_ref),
                (feat_hbm, feat_ref),
                (tiles_ref, tiles),
                (in_w_hbm, weights.at[pl.ds(0, width)]),
                (rec_w_hbm, weights.at[pl.ds(width, hid)]),
                (gcn_w_hbm, gcn_w_ref),
                (gcn_b_hbm, gcn_b_ref),
                (lstm_b_hbm, lstm_b_ref),
                (hgrad_hbm.at[0], hgrad_ref),
            ]
        )
    ]
    for load in loads:
        load.start()
    for s in range(steps):
        fetched[s][nv] = jnp.zeros((tile, width), jnp.bfloat16)
    loads[0].wait()
    for p in range(nv):
        blocks = cols_ref[...] - p * row_blocks
        named = jnp.where((blocks >= 0) & (blocks < row_blocks), blocks, 0)
        for s in range(steps):
            block = jnp.max(named[s], axis=(0, 1), keepdims=True)
            request_ref[p, s] = jnp.broadcast_to(block, (8, LANES))
    pl.semaphore_wait(barrier, ns + nv - 2)

    def ask(k, forward):
        peer = lax.rem(me_v + k, nv) if forward else lax.rem(me_v - k + nv, nv)
        return remote(
            request_ref.at[peer], asked.at[k], ask_sem.at[0, k], ask_sem.at[1, k], "vtx", peer
        )

    def give(k, s, forward):
        peer = lax.rem(me_v + k, nv) if forward else lax.rem(me_v - k + nv, nv)
        return remote(
            staged.at[k, s],
            fetched[s].at[me_v if forward else peer],
            feat_sem.at[0, k, s],
            feat_sem.at[1, k, s],
            "vtx",
            peer,
        )

    for k in range(1, nv):
        ask(k, True).start()
    loads[1].wait()
    for k in range(1, nv):
        ask(nv - k, False).wait_recv()
        wanted = asked[nv - k]
        staged[k, 0] = feat_ref[0, wanted[0, 0, 0]]
        give(k, 0, True).start()
        for s in range(1, steps):
            staged[k, s] = feat_ref[s, wanted[s, 0, 0]]
    own_request = request_ref[me_v]
    for s in range(steps):
        fetched[s][me_v] = feat_ref[s, own_request[s, 0, 0]]
    for load in loads[2:]:
        load.wait()
    weights_t[...] = weights[...].T

    def give_next(s):
        for k in range(1, nv):
            give(k, s - 1, True).wait_send()
            give(k, s, True).start()

    if steps > 1:
        give_next(1)
    hgrad[...] = hgrad_ref[...].astype(jnp.float32).reshape(rows * total_steps, hid)

    def layer_copy(k, s, forward):
        peer = lax.rem(me_s + k, ns) if forward else lax.rem(me_s - k + ns, ns)
        holder = me_s if forward else peer
        return remote(
            layer.at[s, pl.ds(pl.multiple_of(peer * rows, rows), rows)],
            xs.at[holder * steps + s],
            layer_sem.at[0, k, s],
            layer_sem.at[1, k, s],
            "snap",
            peer,
        )

    def convolve(s):
        for k in range(1, nv):
            give(k, s, False).wait_recv()
        if 0 < s < steps - 1:
            give_next(s + 1)
        for r in range(row_blocks):
            picked = [fetched[s][place_ref[s, r, m]] for m in range(slots)]
            left = jnp.concatenate([tiles[s, r, m] for m in range(slots)], axis=1)
            summed = jnp.dot(
                left, jnp.concatenate(picked, axis=0), preferred_element_type=jnp.float32
            )
            aggregated[s, pl.ds(r * tile, tile), :] = summed.astype(jnp.bfloat16)
        pre = (
            jnp.dot(aggregated[s], gcn_w_ref[...], preferred_element_type=jnp.float32)
            + gcn_b_ref[...]
        )
        pre_act[s] = pre
        layer[s] = (pre * sigmoid(pre)).astype(jnp.bfloat16)
        for k in range(1, ns):
            layer_copy(k, s, True).start()
        xs[me_s * steps + s] = layer[s, pl.ds(pl.multiple_of(me_s * rows, rows), rows), :]

    for s in range(steps):
        convolve(s)

    piece = min(rows, LANES)
    hs[0] = jnp.zeros((rows, hid), jnp.bfloat16)
    cells[0] = jnp.zeros((rows, hid), jnp.float32)

    def advance(t, carry):
        holder = lax.div(t, steps)

        @pl.when(holder != me_s)
        def _():
            k = lax.rem(me_s - holder + ns, ns)
            layer_copy(k, lax.rem(t, steps), False).wait_recv()

        for at in range(0, rows, piece):
            here = pl.ds(at, piece)
            both = jnp.concatenate([xs[t, here, :], hs[t, here, :]], axis=1)
            gates = (
                jnp.dot(both, weights[...], preferred_element_type=jnp.float32) + lstm_b_ref[...]
            )
            gate_in = sigmoid(gates[:, :hid])
            gate_keep = sigmoid(gates[:, hid : 2 * hid])
            gate_new = jnp.tanh(gates[:, 2 * hid : 3 * hid])
            gate_out = sigmoid(gates[:, 3 * hid :])
            cell = gate_keep * cells[t, here, :] + gate_in * gate_new
            out = (gate_out * jnp.tanh(cell)).astype(jnp.bfloat16)
            acts[t, 0, here, :] = gate_in
            acts[t, 1, here, :] = gate_keep
            acts[t, 2, here, :] = gate_new
            acts[t, 3, here, :] = gate_out
            cells[t + 1, here, :] = cell
            hs[t + 1, here, :] = out
            place = pl.ds(t + at * total_steps, piece, stride=total_steps)
            hidden[place, :] = out.astype(jnp.float32)
        return carry

    lax.fori_loop(0, total_steps, advance, 0)

    def back_copy(t, peer, forward):
        holder = lax.div(t, steps)
        s = lax.rem(t, steps)
        k = lax.rem(holder - me_s + ns, ns) if forward else lax.rem(me_s - peer + ns, ns)
        sender = me_s if forward else peer
        return remote(
            dlayer.at[t],
            dlayer_in.at[s, pl.ds(pl.multiple_of(sender * rows, rows), rows)],
            back_send.at[t],
            back_recv.at[k, s],
            "snap",
            holder if forward else peer,
        )

    dcell[...] = jnp.zeros((rows, hid), jnp.float32)
    back[...] = jnp.zeros((rows, hid), jnp.float32)
    lstm_b_sum[...] = jnp.zeros(lstm_b_sum.shape, jnp.float32)
    sum1[...] = jnp.zeros(sum1.shape, jnp.float32)
    height = width + hid

    def retreat(step, carry):
        t = total_steps - 1 - step
        parts, grads = [], []
        for at in range(0, rows, piece):
            here = pl.ds(at, piece)
            gate_in, gate_keep, gate_new, gate_out = (acts[t, q, here, :] for q in range(4))
            squash = jnp.tanh(cells[t + 1, here, :])
            place = pl.ds(t + at * total_steps, piece, stride=total_steps)
            dh = hgrad[place, :] + back[here, :]
            dc = dcell[here, :] + dh * gate_out * (1.0 - squash * squash)
            part = jnp.concatenate(
                [
                    dc * gate_new * gate_in * (1.0 - gate_in),
                    dc * cells[t, here, :] * gate_keep * (1.0 - gate_keep),
                    dc * gate_in * (1.0 - gate_new * gate_new),
                    dh * squash * gate_out * (1.0 - gate_out),
                ],
                axis=1,
            ).astype(jnp.bfloat16)
            dcell[here, :] = dc * gate_keep
            both_back = jnp.dot(part, weights_t[...], preferred_element_type=jnp.float32)
            back[here, :] = both_back[:, width:]
            grads.append(both_back[:, :width].astype(jnp.bfloat16))
            parts.append(part)
        grad = jnp.concatenate(grads, axis=0)
        dgates = jnp.concatenate(parts, axis=0)
        holder = lax.div(t, steps)

        @pl.when(holder != me_s)
        def _():
            dlayer[t] = grad
            back_copy(t, None, True).start()

        @pl.when(holder == me_s)
        def _():
            place = pl.ds(pl.multiple_of(me_s * rows, rows), rows)
            dlayer_in[lax.rem(t, steps), place, :] = grad

        lstm_b_sum[...] += jnp.sum(
            dgates.astype(jnp.float32).reshape(rows // 8, 8, 4 * hid), axis=0
        )
        both = jnp.concatenate([xs[t], hs[t]], axis=1)
        term = lax.dot_general(
            both, dgates, (((0,), (0,)), ((), ())), preferred_element_type=jnp.float32
        )
        for q in range(4):
            sum1[q * height : (q + 1) * height, :] += term[:, q * hid : (q + 1) * hid]
        return carry

    lax.fori_loop(0, total_steps, retreat, 0)

    first = Reducer(
        me, sizes, sum1, sent1, part_in1, part1, part_sent1, chunk_in1, whole1, sems1
    )
    second = Reducer(
        me, sizes, sum2, sum2, part_in2, part2, part2, chunk_in2, whole2, sems2
    )
    sent1[...] = sum1[...].astype(jnp.bfloat16)
    first.start(0)
    hid_out[...] = hidden[...].reshape(rows, total_steps, hid).astype(jnp.bfloat16)

    sum2[...] = jnp.zeros(sum2.shape, jnp.float32)
    gcn_b_sum = jnp.zeros((1, width), jnp.float32)
    for s in reversed(range(steps)):
        for k in range(1, ns):
            src = lax.rem(me_s - k + ns, ns)
            back_copy(me_s * steps + s, src, False).wait_recv()
        pre = pre_act[s]
        slope = sigmoid(pre)
        dpre = (dlayer_in[s].astype(jnp.float32) * slope * (1.0 + pre * (1.0 - slope))).astype(
            jnp.bfloat16
        )
        sum2[:width, :] += lax.dot_general(
            aggregated[s], dpre, (((0,), (0,)), ((), ())), preferred_element_type=jnp.float32
        )
        gcn_b_sum = gcn_b_sum + jnp.sum(dpre.astype(jnp.float32), axis=0, keepdims=True)
    lstm_b = jnp.sum(lstm_b_sum[...], axis=0, keepdims=True)
    sum2[width : width + 1, :] = gcn_b_sum
    for q in range(4):
        sum2[width + 1 + q : width + 2 + q, :] = lstm_b[:, q * hid : (q + 1) * hid]

    second.start(0)
    for stage in range(4):
        first.finish(stage)
        if stage < 3:
            first.start(stage + 1)
        second.finish(stage)
        if stage < 3:
            second.start(stage + 1)

    for q in range(4):
        at = q * height
        span = slice(q * hid, (q + 1) * hid)
        in_out[:, span] = whole1[at : at + width, :].astype(jnp.float32)
        rec_out[:, span] = whole1[at + width : at + height, :].astype(jnp.float32)
        lstm_b_out[:, span] = whole2[width + 1 + q : width + 2 + q, :]
    gcn_out[...] = whole2[:width, :]
    gcn_b_out[...] = whole2[width : width + 1, :]

    for k in range(1, nv):
        ask(k, True).wait_send()
        give(k, steps - 1, True).wait_send()
    for k in range(1, ns):
        for s in range(steps):
            layer_copy(k, s, True).wait_send()

    def drain(t, carry):
        @pl.when(lax.div(t, steps) != me_s)
        def _():
            back_copy(t, None, True).wait_send()

        return carry

    lax.fori_loop(0, total_steps, drain, 0)
    first.drain()
    second.drain()


def write_out(*refs):
    *arrays, sems = refs
    n = len(arrays) // 3
    srcs, dsts, held = arrays[:n], arrays[n : 2 * n], arrays[2 * n :]
    ins = [pltpu.make_async_copy(srcs[i], held[i], sems.at[0, i]) for i in range(n)]
    outs = [pltpu.make_async_copy(held[i], dsts[i], sems.at[1, i]) for i in range(n)]
    for copy in ins:
        copy.start()
    for copy_in, copy_out in zip(ins, outs):
        copy_in.wait()
        copy_out.start()
    for copy in outs:
        copy.wait()


def on_device(
    sizes,
    features,
    tile_vals,
    tile_cols,
    tile_count,
    gcn_weight,
    gcn_bias,
    input_weight,
    recur_weight,
    lstm_bias,
    hidden_grad,
):
    ns, nv = sizes["snap"], sizes["vtx"]
    steps, verts, width = features.shape
    _, row_blocks, slots, tile, _ = tile_vals.shape
    hid = recur_weight.shape[0]
    _, rows, total_steps, _ = hidden_grad.shape
    bf16, f32 = jnp.bfloat16, jnp.float32

    live = lax.broadcasted_iota(jnp.int32, tile_cols.shape, 2) < tile_count[:, :, None]
    places = jnp.where(live, tile_cols // row_blocks, nv)

    def padded(count, unit):
        unit = unit * ns * nv
        return -(-count // unit) * unit

    rows1 = padded(4 * (width + hid), 16)
    rows2 = padded(width + 5, 8)
    most = max(ns, nv)
    dma = pltpu.SemaphoreType.DMA

    def reduction(count, kept):
        part = count // ns
        return [
            pltpu.VMEM((count, LANES), f32),
            pltpu.VMEM((ns - 1, part, LANES), kept),
            pltpu.VMEM((part, LANES), f32),
            pltpu.VMEM((nv - 1, part // nv, LANES), kept),
            pltpu.VMEM((count, LANES), kept),
        ]

    scratch = [
        pltpu.VMEM(tile_vals.shape, bf16),
        pltpu.VMEM(tile_cols.shape, jnp.int32),
        pltpu.VMEM((nv, steps, 8, LANES), jnp.int32),
        pltpu.VMEM((steps, row_blocks, tile, width), bf16),
        pltpu.VMEM(gcn_weight.shape, bf16),
        pltpu.VMEM((1, width), f32),
        pltpu.VMEM((1, 4 * hid), f32),
        pltpu.VMEM((rows, total_steps, hid), bf16),
        pltpu.VMEM((rows * total_steps, hid), f32),
        pltpu.VMEM((rows * total_steps, hid), f32),
        pltpu.VMEM((nv, steps, 8, LANES), jnp.int32),
        pltpu.VMEM((nv, steps, tile, width), bf16),
        [pltpu.VMEM((nv + 1, tile, width), bf16) for _ in range(steps)],
        pltpu.VMEM((steps, verts, width), bf16),
        pltpu.VMEM((steps, verts, width), f32),
        pltpu.VMEM((steps, verts, width), bf16),
        pltpu.VMEM((total_steps, rows, width), bf16),
        pltpu.VMEM((total_steps + 1, rows, hid), bf16),
        pltpu.VMEM((total_steps, 4, rows, hid), f32),
        pltpu.VMEM((total_steps + 1, rows, hid), f32),
        pltpu.VMEM((total_steps, rows, width), bf16),
        pltpu.VMEM((steps, verts, width), bf16),
        pltpu.VMEM((rows, hid), f32),
        pltpu.VMEM((rows, hid), f32),
        pltpu.VMEM((width + hid, 4 * hid), bf16),
        pltpu.VMEM((4 * hid, width + hid), bf16),
        pltpu.VMEM((8, 4 * hid), f32),
        *reduction(rows1, bf16),
        pltpu.VMEM((rows1, LANES), bf16),
        pltpu.VMEM((rows1 // ns, LANES), bf16),
        *reduction(rows2, f32),
        dma((9,)),
        dma((2, nv)),
        dma((2, nv, steps)),
        dma((2, ns, steps)),
        dma((total_steps,)),
        dma((ns, steps)),
        dma((8, most)),
        dma((8, most)),
    ]
    vmem = pl.BlockSpec(memory_space=pltpu.VMEM)
    smem = pl.BlockSpec(memory_space=pltpu.SMEM)
    hbm = pl.BlockSpec(memory_space=pl.ANY)
    results = pl.pallas_call(
        functools.partial(kernel, sizes),
        out_shape=[
            jax.ShapeDtypeStruct((rows, total_steps, hid), bf16),
            jax.ShapeDtypeStruct((width, width), f32),
            jax.ShapeDtypeStruct((1, width), f32),
            jax.ShapeDtypeStruct((width, 4 * hid), f32),
            jax.ShapeDtypeStruct((hid, 4 * hid), f32),
            jax.ShapeDtypeStruct((1, 4 * hid), f32),
        ],
        in_specs=[hbm, smem] + [hbm] * 8,
        out_specs=[vmem] * 6,
        scratch_shapes=scratch,
        compiler_params=pltpu.CompilerParams(
            collective_id=0, has_side_effects=True, vmem_limit_bytes=60 * 2**20
        ),
    )(
        tile_cols,
        places,
        features.reshape(steps, row_blocks, tile, width),
        tile_vals,
        gcn_weight,
        gcn_bias.reshape(1, -1),
        input_weight,
        recur_weight,
        lstm_bias.reshape(1, -1),
        hidden_grad,
    )
    count = len(results)
    hidden, grad_gcn, grad_gbias, grad_input, grad_recur, grad_bias = pl.pallas_call(
        write_out,
        out_shape=[jax.ShapeDtypeStruct(each.shape, each.dtype) for each in results],
        in_specs=[hbm] * count,
        out_specs=[hbm] * count,
        scratch_shapes=[pltpu.VMEM(each.shape, each.dtype) for each in results]
        + [dma((2, count))],
        compiler_params=pltpu.CompilerParams(vmem_limit_bytes=60 * 2**20),
    )(*results)
    hidden_states = hidden[None]
    return (
        hidden_states,
        grad_gcn,
        grad_gbias.reshape(-1),
        grad_input,
        grad_recur,
        grad_bias.reshape(-1),
    )


def solution(mesh):
    sizes = {axis: mesh.shape[axis] for axis in ("snap", "vtx")}
    return jax.shard_map(
        functools.partial(on_device, sizes),
        mesh=mesh,
        in_specs=(
            P("snap", "vtx", None),
            P("snap", "vtx", None, None, None),
            P("snap", "vtx", None),
            P("snap", "vtx"),
            P(),
            P(),
            P(),
            P(),
            P(),
            P("vtx", "snap", None, None),
        ),
        out_specs=(P("vtx", "snap", None, None), P(), P(), P(), P(), P()),
        check_vma=False,
    )
```
